32 devices in a mesh: expert: 8 (over z, y), replica: 4 (over x, core).
Axes of the slice: x: 2, y: 2, z: 4, core: 2. Of those that a mesh axis runs over, the one named last changes fastest.
Arguments:
- inputs: bfloat16 [2, 2048, 2048], P(None, ('expert', 'replica')), may hold values from -6 to 6
- out_grads: bfloat16 [2, 2048, 2048], P(None, ('expert', 'replica')), may hold values from -6 to 6
- routes: int32 [2, 2048, 1], P(None, ('expert', 'replica')), may hold values from 0 to 7; in each aligned block of 64 rows (0 to 63, 64 to 127, ..., all dimensions but the last counted through in order) at most 16 rows name the same one
- gate_probs: float32 [2, 2048, 1], P(None, ('expert', 'replica')), may hold values from 0.2 to 1
- master: float32 [8, 256, 6144], P('expert', 'replica'), may hold values from -6 to 6
- moment: float32 [8, 256, 6144], P('expert', 'replica'), may hold values from -3 to 3
- second: bfloat16 [8, 256, 6144], P('expert', 'replica'), may hold values from 0.0099487305 to 1
Outputs:
- in_grads: bfloat16 [2, 2048, 2048], P(None, ('expert', 'replica'))
- new_master: float32 [8, 256, 6144], P('expert', 'replica')
- new_moment: float32 [8, 256, 6144], P('expert', 'replica')
- new_second: bfloat16 [8, 256, 6144], P('expert', 'replica')
The draws below stay inside these ranges and needn't reach their ends.
Inputs may be any that keep to these rules, and one draw needn't show every extreme that they name: `routes`: each token names exactly one expert. In each micro-batch no expert is named by more than 16 tokens of one block of 64 tokens, a bound that some block reaches.
All inputs are finite; a program needn't handle non-finite values.
Results may differ from the reference program's by a relative error of at most 0.028.
Values may be sent and summed in bfloat16 or wider, within the bound.
A program may use at most 64 MiB of HBM per device.

```python
import math
import jax
import jax.numpy as jnp
import numpy as np
from jax import lax

D = 2048
FF = 256
TOPK = 1
MB = 2
TOK = 64
EXPERTS = 8
CAP = 16
TOKENS = 2048
N_REPLICA = 4


def block_levels(rng, dims, pieces, least, largest):
    level = 1.0
    for dim, shards_of in pieces:
        steps = jax.random.uniform(jax.random.fold_in(jax.random.fold_in(rng, 6), dim), (shards_of,), jnp.float32, least / len(pieces), largest / len(pieces))
        level = level * jnp.repeat(jnp.exp(steps), dims[dim] // shards_of).reshape((-1,) + (1,) * (len(dims) - 1 - dim))
    return level


def routed_block(rng, own, number, rows, amount, top, most, skew):
    order = jax.random.permutation(rng, amount)
    heavy_load, common = load_shares(amount, rows * top, most, skew, True), load_shares(amount, rows * top, most, skew, False)
    places = jnp.arange(amount)

    def named(lengths, turn):
        used = int((lengths > 0).sum())
        fixed = max(1, used // 4)
        passed = fixed + (places - fixed + turn * (used - fixed)) % max(1, amount - fixed)
        return jnp.zeros((amount,), jnp.int32).at[order[jnp.where(places < fixed, places, passed)]].set(jnp.asarray(lengths, jnp.int32))

    lengths = jnp.where(number % 4 == 0, named(heavy_load, number // 4), named(common, number - number // 4 - 1))
    mixed = jax.random.permutation(jax.random.fold_in(own, 3), amount)
    donor, taker = mixed[0:amount // 2 * 2:2], mixed[1:amount // 2 * 2:2]
    slack = jnp.minimum(lengths[donor] - 1, most - lengths[taker]) // 2
    slack = jnp.where((donor == order[0]) | (taker == order[0]) | (lengths[taker] == 0), 0, jnp.maximum(slack, 0))
    passed = jax.random.randint(jax.random.fold_in(own, 4), (amount // 2,), 0, 1 << 20) % (slack + 1)
    lengths = lengths.at[donor].add(-passed).at[taker].add(passed)
    members = jnp.searchsorted(jnp.cumsum(lengths), jnp.arange(rows * top), side="right").astype(jnp.int32)
    grid = members.reshape(top, rows).T
    grid = grid[jax.random.permutation(jax.random.fold_in(own, 1), rows)]
    turn = jax.random.randint(jax.random.fold_in(own, 2), (rows, 1), 0, top)
    return jnp.take_along_axis(grid, (jnp.arange(top)[None, :] + turn) % top, axis=1)


def load_shares(amount, total, bound, skew, full):
    loads = [(1 << 20) // math.isqrt(rank ** skew) + 1 for rank in range(1, amount + 1)]
    largest = bound if full else min(bound, max(-(-total // amount), total * loads[0] // sum(loads)))
    least = 1 if total - largest >= amount - 1 else 0
    counts, spare = [largest] + [least] * (amount - 1), total - largest - least * (amount - 1)
    while spare > 0:
        free = [i for i in range(1, amount) if counts[i] < largest] or [i for i in range(1, amount) if counts[i] < bound]
        pool, left = sum([loads[i] for i in free]), spare
        for i in free:
            more = min(bound - counts[i], max(1, left * loads[i] // pool), spare)
            counts[i] = counts[i] + more
            spare = spare - more
    return np.array(counts)


def centred(stream_key, dims, spread, limit, pieces=(), held_as=jnp.bfloat16):
    entries = jax.random.normal(stream_key, dims, jnp.float32) * spread
    if len(pieces) > 0:
        entries = block_levels(stream_key, dims, pieces, -0.22, 0.18) * entries
    return jnp.clip(entries, min=-limit, max=limit).astype(held_as)


def setup_inputs(seed: int = 0) -> dict:
    arg_keys = jax.random.split(jax.random.key(seed), 8)
    inputs = centred(arg_keys[0], (MB, TOKENS, D), 1.0, 6.0, ((1, 32),))
    out_grads = centred(arg_keys[1], (MB, TOKENS, D), 1.0, 6.0, ((1, 32),))
    routes_keys = jax.random.split(jax.random.fold_in(arg_keys[2], 1), MB * TOKENS // TOK)
    routes_turns = jax.random.permutation(jax.random.fold_in(arg_keys[2], 3), MB * TOKENS // TOK)
    routes = jax.vmap(lambda own, number: routed_block(jax.random.fold_in(arg_keys[2], 2), own, number, TOK, EXPERTS, TOPK, CAP, 2))(routes_keys, routes_turns).reshape((MB, TOKENS, TOPK))
    gate_probs = jnp.clip(0.2 + 0.8 * jax.random.uniform(arg_keys[3], (MB, TOKENS, TOPK), jnp.float32) ** block_levels(arg_keys[3], (MB, TOKENS, TOPK), ((1, 32),), -0.2, 0.2), 0.2, 1.0)
    master = centred(arg_keys[4], (EXPERTS, FF, 3 * D), 1.0, 6.0, ((0, 8), (1, 4)), jnp.float32)
    moment = centred(arg_keys[5], (EXPERTS, FF, 3 * D), 0.3, 3.0, ((0, 8), (1, 4)), jnp.float32)
    second = jnp.clip(jnp.exp(math.log(1.0) - 4.61031033 * jax.random.uniform(arg_keys[6], (EXPERTS, FF, 3 * D), jnp.float32) ** block_levels(arg_keys[6], (EXPERTS, FF, 3 * D), ((0, 8), (1, 4)), -0.2, 0.2)), 0.0099487305, 1.0).astype(jnp.bfloat16)
    return {"inputs": inputs, "out_grads": out_grads, "routes": routes, "gate_probs": gate_probs, "master": master, "moment": moment, "second": second}


beta_one = 0.9
beta_two = 0.95
learning_rate = 0.01
decay_rate = 0.1
epsilon = 1e-08

def slot_positions(route_pairs, capacity):
    pair_count = route_pairs.shape[-1]
    positions = jnp.arange(pair_count, dtype=jnp.int32)
    same_route = (route_pairs[..., :, None] == route_pairs[..., None, :]) & (positions[None, :] < positions[:, None])
    earlier = lax.optimization_barrier(jnp.sum(same_route.astype(jnp.int32), axis=-1))
    return route_pairs * capacity + earlier

def expert_rows(rows_in, rows_grad, weights):
    model_width = rows_in.shape[-1]
    scale_in = 1.0 / math.sqrt(model_width)
    scale_hidden = 1.0 / math.sqrt(weights.shape[0])
    w_gate = weights[:, :model_width]
    w_up = weights[:, model_width:2 * model_width]
    w_down = weights[:, 2 * model_width:]
    gate_value = jnp.dot(rows_in, w_gate.T, preferred_element_type=jnp.float32) * scale_in
    up_value = jnp.dot(rows_in, w_up.T, preferred_element_type=jnp.float32) * scale_in
    sigmoid_gate = jax.nn.sigmoid(gate_value)
    activated = gate_value * sigmoid_gate
    hidden = (activated * up_value).astype(jnp.bfloat16)
    hidden_grad = jnp.dot(rows_grad, w_down.T, preferred_element_type=jnp.float32) * scale_hidden
    up_grad = (hidden_grad * activated).astype(jnp.bfloat16)
    gate_grad = (hidden_grad * up_value * sigmoid_gate * (1.0 + gate_value * (1.0 - sigmoid_gate))).astype(jnp.bfloat16)
    slot_grads = (jnp.dot(gate_grad, w_gate, preferred_element_type=jnp.float32) + jnp.dot(up_grad, w_up, preferred_element_type=jnp.float32)) * scale_in
    return (hidden, gate_grad, up_grad, slot_grads.astype(jnp.bfloat16))

def gate_up_terms(rows_in, gate_grad, up_grad, first_row, row_count):
    scale_in = 1.0 / math.sqrt(rows_in.shape[-1])
    gate_cols = lax.dynamic_slice_in_dim(gate_grad, first_row, row_count, 1)
    up_cols = lax.dynamic_slice_in_dim(up_grad, first_row, row_count, 1)
    gate_term = jnp.dot(gate_cols.T, rows_in, preferred_element_type=jnp.float32) * scale_in
    up_term = jnp.dot(up_cols.T, rows_in, preferred_element_type=jnp.float32) * scale_in
    return jnp.concatenate([gate_term, up_term], axis=1)

def down_terms(rows_grad, hidden, first_row, row_count):
    scale_hidden = 1.0 / math.sqrt(hidden.shape[-1])
    hidden_cols = lax.dynamic_slice_in_dim(hidden, first_row, row_count, 1)
    return jnp.dot(hidden_cols.T, rows_grad, preferred_element_type=jnp.float32) * scale_hidden

def adamw_step(master, moment, second, grad_sum):
    new_moment = beta_one * moment + (1.0 - beta_one) * grad_sum
    second_sum = beta_two * second.astype(jnp.float32) + (1.0 - beta_two) * grad_sum * grad_sum
    new_master = master - learning_rate * (new_moment / (jnp.sqrt(second_sum) + epsilon) + decay_rate * master)
    return (new_master, new_moment, second_sum.astype(jnp.bfloat16))

def replica_terms(operands):
    rows_in, rows_grad, hidden, gate_grad, up_grad = operands
    hidden_units = hidden.shape[-1]
    gate_up = gate_up_terms(rows_in, gate_grad, up_grad, 0, hidden_units)
    down = down_terms(rows_grad, hidden, 0, hidden_units)
    return jnp.concatenate([gate_up, down], axis=1).astype(jnp.bfloat16)

def reference(inputs, out_grads, routes, gate_probs, master, moment, second):
    blocks = EXPERTS * N_REPLICA
    pair_count = TOK * TOPK
    route_pairs = routes.reshape(MB, blocks, pair_count)
    slot_ids = slot_positions(route_pairs, CAP)
    batch_ids = jnp.arange(MB, dtype=jnp.int32)[:, None, None]
    block_ids = jnp.arange(blocks, dtype=jnp.int32)[None, :, None]
    pair_ids = jnp.broadcast_to(jnp.arange(pair_count, dtype=jnp.int32)[None, None, :], slot_ids.shape)
    slot_table = jnp.full((MB, blocks, EXPERTS * CAP), -1, jnp.int32).at[batch_ids, block_ids, slot_ids].set(pair_ids)
    rows_each = MB * EXPERTS * CAP

    def per_expert(expert):
        expert_table = lax.dynamic_slice_in_dim(slot_table, expert * CAP, CAP, 2)
        filled = expert_table >= 0
        pair_index = jnp.maximum(expert_table, 0)
        token_ids = block_ids * TOK + pair_index // TOPK
        choice_ids = pair_index % TOPK
        rows_in = jnp.where(filled[..., None], inputs[batch_ids, token_ids], jnp.zeros((), jnp.bfloat16))
        pair_prob = gate_probs[batch_ids, token_ids, choice_ids]
        scaled = pair_prob[..., None] * out_grads[batch_ids, token_ids].astype(jnp.float32)
        rows_grad = jnp.where(filled[..., None], scaled, jnp.zeros((), jnp.float32)).astype(jnp.bfloat16)
        weights = lax.dynamic_index_in_dim(master, expert, 0, keepdims=False).astype(jnp.bfloat16)
        rows_in = rows_in.reshape(MB, EXPERTS, N_REPLICA, CAP, D).transpose(2, 0, 1, 3, 4).reshape(N_REPLICA * rows_each, D)
        rows_grad = rows_grad.reshape(MB, EXPERTS, N_REPLICA, CAP, D).transpose(2, 0, 1, 3, 4).reshape(N_REPLICA * rows_each, D)
        hidden, gate_grad, up_grad, slot_grads = expert_rows(rows_in, rows_grad, weights)
        partial_value = lax.map(replica_terms, (rows_in.reshape(N_REPLICA, rows_each, D), rows_grad.reshape(N_REPLICA, rows_each, D), hidden.reshape(N_REPLICA, rows_each, FF), gate_grad.reshape(N_REPLICA, rows_each, FF), up_grad.reshape(N_REPLICA, rows_each, FF)))
        grad_sum = lax.optimization_barrier(jnp.sum(partial_value.astype(jnp.float32), axis=0))
        slot_grads = slot_grads.reshape(N_REPLICA, MB, EXPERTS, CAP, D).transpose(1, 2, 0, 3, 4).reshape(MB, blocks, CAP, D)
        return (slot_grads, grad_sum)
    all_slots, grads = lax.map(per_expert, jnp.arange(EXPERTS, dtype=jnp.int32))
    earlier = slot_ids % CAP
    pair_grads = all_slots[route_pairs, batch_ids, block_ids, earlier]
    in_grads = lax.optimization_barrier(jnp.sum(pair_grads.astype(jnp.float32).reshape(MB, blocks, TOK, TOPK, D), axis=3))
    in_grads = in_grads.astype(jnp.bfloat16).reshape(MB, TOKENS, D)
    new_master, new_moment, new_second = adamw_step(master, moment, second, grads)
    return (in_grads, new_master, new_moment, new_second)
```

```python
import functools
import math

import jax
import jax.numpy as jnp
from jax import lax
from jax.experimental import pallas as pl
from jax.experimental.pallas import tpu as pltpu
from jax.sharding import PartitionSpec as P

beta_one = 0.9
beta_two = 0.95
learning_rate = 0.01
decay_rate = 0.1
epsilon = 1e-08
MESH = pl.DeviceIdType.MESH
NT = (((1,), (1,)), ((), ()))


def slot_positions(route_pairs, capacity):
    pair_count = route_pairs.shape[-1]
    positions = jnp.arange(pair_count, dtype=jnp.int32)
    same_route = (route_pairs[..., :, None] == route_pairs[..., None, :]) & (
        positions[None, :] < positions[:, None]
    )
    earlier = jnp.sum(same_route.astype(jnp.int32), axis=-1)
    return route_pairs * capacity + earlier


def expert_rows(rows_in, rows_grad, weights):
    model_width = rows_in.shape[-1]
    scale_in = 1.0 / math.sqrt(model_width)
    scale_hidden = 1.0 / math.sqrt(weights.shape[0])
    w_gate = weights[:, :model_width]
    w_up = weights[:, model_width : 2 * model_width]
    w_down = weights[:, 2 * model_width :]
    gate_value = jnp.dot(rows_in, w_gate.T, preferred_element_type=jnp.float32) * scale_in
    up_value = jnp.dot(rows_in, w_up.T, preferred_element_type=jnp.float32) * scale_in
    sigmoid_gate = jax.nn.sigmoid(gate_value)
    activated = gate_value * sigmoid_gate
    hidden = (activated * up_value).astype(jnp.bfloat16)
    hidden_grad = jnp.dot(rows_grad, w_down.T, preferred_element_type=jnp.float32) * scale_hidden
    up_grad = (hidden_grad * activated).astype(jnp.bfloat16)
    gate_grad = (
        hidden_grad * up_value * sigmoid_gate * (1.0 + gate_value * (1.0 - sigmoid_gate))
    ).astype(jnp.bfloat16)
    slot_grads = (
        jnp.dot(gate_grad, w_gate, preferred_element_type=jnp.float32)
        + jnp.dot(up_grad, w_up, preferred_element_type=jnp.float32)
    ) * scale_in
    return (hidden, gate_grad, up_grad, slot_grads.astype(jnp.bfloat16))


def gate_up_terms(rows_in, gate_grad, up_grad):
    scale_in = 1.0 / math.sqrt(rows_in.shape[-1])
    gate_term = jnp.dot(gate_grad.T, rows_in, preferred_element_type=jnp.float32) * scale_in
    up_term = jnp.dot(up_grad.T, rows_in, preferred_element_type=jnp.float32) * scale_in
    return jnp.concatenate([gate_term, up_term], axis=1)


def down_terms(rows_grad, hidden):
    scale_hidden = 1.0 / math.sqrt(hidden.shape[-1])
    return jnp.dot(hidden.T, rows_grad, preferred_element_type=jnp.float32) * scale_hidden


def adamw_step(master, moment, second, grad_sum):
    new_moment = beta_one * moment + (1.0 - beta_one) * grad_sum
    second_sum = beta_two * second.astype(jnp.float32) + (1.0 - beta_two) * grad_sum * grad_sum
    new_master = master - learning_rate * (
        new_moment / (jnp.sqrt(second_sum) + epsilon) + decay_rate * master
    )
    return (new_master, new_moment, second_sum.astype(jnp.bfloat16))


def on_device_plain(inputs, out_grads, routes, gate_probs, master, moment, second):
    experts = lax.axis_size("expert")
    batches, tokens, model_width = inputs.shape
    top_count = routes.shape[2]
    pair_count = tokens * top_count
    capacity = max(2, 2 * pair_count // experts)
    weights = lax.all_gather(master[0].astype(jnp.bfloat16), "replica", axis=0, tiled=True)
    route_pairs = routes.reshape(batches, pair_count)
    slot_ids = slot_positions(route_pairs, capacity)
    slot_range = jnp.arange(experts * capacity, dtype=jnp.int32)
    onehot = (slot_ids[:, None, :] == slot_range[None, :, None]).astype(jnp.bfloat16)
    onehot = onehot.reshape(batches, experts, capacity, pair_count)
    pair_inputs = jnp.repeat(inputs, top_count, axis=1)
    pair_grads = (
        gate_probs.reshape(batches, pair_count)[..., None]
        * jnp.repeat(out_grads, top_count, axis=1).astype(jnp.float32)
    ).astype(jnp.bfloat16)
    send_in = jnp.einsum(
        "besp,bpd->ebsd", onehot, pair_inputs, preferred_element_type=jnp.float32
    ).astype(jnp.bfloat16)
    send_grad = jnp.einsum(
        "besp,bpd->ebsd", onehot, pair_grads, preferred_element_type=jnp.float32
    ).astype(jnp.bfloat16)
    arrived_in, arrived_grad = (
        lax.all_to_all(send_in, "expert", split_axis=0, concat_axis=0, tiled=True),
        lax.all_to_all(send_grad, "expert", split_axis=0, concat_axis=0, tiled=True),
    )
    all_in = arrived_in.reshape(experts * batches * capacity, model_width)
    all_grad = arrived_grad.reshape(experts * batches * capacity, model_width)
    all_hidden, all_gate, all_up, slot_grads = expert_rows(all_in, all_grad, weights)
    returned_rows = lax.all_to_all(
        slot_grads.reshape(experts, batches, capacity, model_width),
        "expert",
        split_axis=0,
        concat_axis=0,
        tiled=True,
    )
    pair_back = jnp.einsum(
        "besp,ebsd->bpd", onehot, returned_rows, preferred_element_type=jnp.float32
    )
    in_grads = jnp.sum(pair_back.reshape(batches, tokens, top_count, model_width), axis=2).astype(
        jnp.bfloat16
    )
    grad_sum = lax.psum_scatter(
        jnp.concatenate(
            [gate_up_terms(all_in, all_gate, all_up), down_terms(all_grad, all_hidden)], axis=1
        ).astype(jnp.bfloat16),
        "replica",
        scatter_dimension=0,
        tiled=True,
    ).astype(jnp.float32)
    new_master, new_moment, new_second = adamw_step(master[0], moment[0], second[0], grad_sum)
    return (in_grads, new_master[None], new_moment[None], new_second[None])


def layer_kernel(
    experts,
    capacity,
    in_ref,
    og_ref,
    routes_ref,
    probs_ref,
    master_ref,
    ingrad_ref,
    grad_ref,
    send,
    recv,
    weights,
    slots,
    ret,
    pick_back,
    terms,
    part,
    sib,
    chip_sum,
    from_x,
    dsend,
    drecv,
    bsend,
    brecv,
    wsend,
    wrecv,
    rsend,
    rrecv,
):
    batches, tokens, width = in_ref.shape
    units = weights.shape[2]
    total_units = 4 * units
    rows = experts * capacity
    scale_in = 1.0 / math.sqrt(width)
    scale_hidden = 1.0 / math.sqrt(total_units)
    e = lax.axis_index("expert")
    r = lax.axis_index("replica")
    chip_x, core = r // 2, lax.rem(r, 2)
    r_sib = chip_x * 2 + (1 - core)
    r_x = (1 - chip_x) * 2 + core
    r_far = (1 - chip_x) * 2 + (1 - core)

    barrier = pltpu.get_barrier_semaphore()

    def greet(k, c):
        pl.semaphore_signal(
            barrier, inc=1, device_id=(lax.rem(e + k, experts), r), device_id_type=MESH
        )
        return c

    lax.fori_loop(1, experts, greet, 0)
    for other in (r_sib, r_x):
        pl.semaphore_signal(barrier, inc=1, device_id=(e, other), device_id_type=MESH)

    def dispatch(which, b, k):
        peer = lax.rem(e + k, experts)
        return pltpu.make_async_remote_copy(
            src_ref=send.at[which, b, peer],
            dst_ref=recv.at[which, b, e],
            send_sem=dsend.at[which, b, k - 1],
            recv_sem=drecv.at[which, b, k - 1],
            device_id=(peer, r),
            device_id_type=MESH,
        )

    def give_back(b, k):
        peer = lax.rem(e + k, experts)
        return pltpu.make_async_remote_copy(
            src_ref=slots.at[b, peer],
            dst_ref=ret.at[b, e],
            send_sem=bsend.at[b, k - 1],
            recv_sem=brecv.at[b, k - 1],
            device_id=(peer, r),
            device_id_type=MESH,
        )

    def weight_copy(kind, k):
        block = (r, r, r_x)[kind]
        target = (r_sib, r_x, r_sib)[kind]
        return pltpu.make_async_remote_copy(
            src_ref=weights.at[k, block],
            dst_ref=weights.at[k, block],
            send_sem=wsend.at[kind, k],
            recv_sem=wrecv.at[kind, k],
            device_id=(e, target),
            device_id_type=MESH,
        )

    def grad_copy(kind, k):
        if kind == 2:
            source, target, place = chip_sum.at[k], r_x, from_x.at[k]
        else:
            source, target = part.at[k, (r_far, r_sib)[kind]], r_sib
            place = sib.at[kind, k]
        return pltpu.make_async_remote_copy(
            src_ref=source,
            dst_ref=place,
            send_sem=rsend.at[kind, k],
            recv_sem=rrecv.at[kind, k],
            device_id=(e, target),
            device_id_type=MESH,
        )

    def each_peer(step):
        def body(k, c):
            step(k)
            return c

        lax.fori_loop(1, experts, body, 0)

    first = lax.broadcasted_iota(jnp.int32, (tokens, tokens), 0)
    second = lax.broadcasted_iota(jnp.int32, (tokens, tokens), 1)

    def pick(b):
        route_col = routes_ref[b].astype(jnp.float32)
        route_row = jnp.sum(jnp.where(first == second, route_col, 0.0), axis=0, keepdims=True)
        same = route_col == route_row
        before_row = jnp.sum(
            jnp.where(same & (first < second), 1.0, 0.0), axis=0, keepdims=True
        )
        before_col = jnp.sum(
            jnp.where(same & (second < first), 1.0, 0.0), axis=1, keepdims=True
        )
        slot_row = route_row * capacity + before_row
        slot_col = route_col * capacity + before_col
        by_slot = lax.broadcasted_iota(jnp.int32, (rows, tokens), 0).astype(jnp.float32)
        by_token = lax.broadcasted_iota(jnp.int32, (tokens, rows), 1).astype(jnp.float32)
        one_hot = jnp.where(by_slot == slot_row, 1.0, 0.0).astype(jnp.bfloat16)
        pick_back[b] = jnp.where(by_token == slot_col, 1.0, 0.0).astype(jnp.bfloat16)
        return one_hot

    def fill(which, b, one_hot):
        if which == 0:
            source = in_ref[b]
        else:
            source = (probs_ref[b] * og_ref[b].astype(jnp.float32)).astype(jnp.bfloat16)
        chosen = jnp.dot(one_hot, source, preferred_element_type=jnp.float32)
        send[which, b] = chosen.astype(jnp.bfloat16).reshape(experts, capacity, width)
        recv[which, b, e] = send[which, b, e]

    one_hot = pick(0)
    fill(0, 0, one_hot)
    pl.semaphore_wait(barrier, experts + 1)
    each_peer(lambda k: dispatch(0, 0, k).start())
    for k in range(3):
        weights[k, r] = master_ref[:, k * width : (k + 1) * width].astype(jnp.bfloat16)
        weight_copy(1, k).start()
        weight_copy(0, k).start()
    fill(1, 0, one_hot)
    each_peer(lambda k: dispatch(1, 0, k).start())
    for b in range(1, batches):
        one_hot = pick(b)
        for which in range(2):
            fill(which, b, one_hot)
            each_peer(lambda k: dispatch(which, b, k).start())

    for k in range(3):
        weight_copy(1, k).wait_recv()
        weight_copy(2, k).start()
    for k in range(3):
        weight_copy(0, k).wait_recv()
        weight_copy(2, k).wait_recv()

    def matrix(k):
        return weights[k].reshape(total_units, width)

    for b in range(batches):
        each_peer(lambda k: dispatch(0, b, k).wait_recv())
        x = recv[0, b].reshape(rows, width)
        gate = lax.dot_general(x, matrix(0), NT, preferred_element_type=jnp.float32) * scale_in
        up = lax.dot_general(x, matrix(1), NT, preferred_element_type=jnp.float32) * scale_in
        sig = jax.nn.sigmoid(gate)
        act = gate * sig
        each_peer(lambda k: dispatch(1, b, k).wait_recv())
        g = recv[1, b].reshape(rows, width)
        hgrad = (
            lax.dot_general(g, matrix(2), NT, preferred_element_type=jnp.float32) * scale_hidden
        )
        up_grad = hgrad * act
        gate_grad = hgrad * up * sig * (1.0 + gate * (1.0 - sig))
        gate_low, up_low = gate_grad.astype(jnp.bfloat16), up_grad.astype(jnp.bfloat16)
        back = (
            jnp.dot(gate_low, matrix(0), preferred_element_type=jnp.float32)
            + jnp.dot(up_low, matrix(1), preferred_element_type=jnp.float32)
        ) * scale_in
        slots[b] = back.astype(jnp.bfloat16).reshape(experts, capacity, width)
        each_peer(lambda k: give_back(b, k).start())
        ret[b, e] = slots[b, e]
        span = slice(b * rows, (b + 1) * rows)
        terms[0, :, span] = gate_grad.T.astype(jnp.bfloat16)
        terms[1, :, span] = up_grad.T.astype(jnp.bfloat16)
        terms[2, :, span] = (act * up).T.astype(jnp.bfloat16)

    for k in range(3):
        source = recv[k // 2].reshape(batches * rows, width)
        total = jnp.dot(terms[k], source, preferred_element_type=jnp.float32)
        total = total * (scale_hidden if k == 2 else scale_in)
        part[k] = total.astype(jnp.bfloat16).reshape(4, units, width)
        grad_copy(0, k).start()
        grad_copy(1, k).start()
    for k in range(3):
        grad_copy(0, k).wait_recv()
        chip_sum[k] = (
            part[k, r_x].astype(jnp.float32) + sib[0, k].astype(jnp.float32)
        ).astype(jnp.bfloat16)
        grad_copy(2, k).start()

    for b in range(batches):
        each_peer(lambda k: give_back(b, k).wait_recv())
        back = jnp.dot(
            pick_back[b], ret[b].reshape(rows, width), preferred_element_type=jnp.float32
        )
        ingrad_ref[b] = back.astype(jnp.bfloat16)
    for k in range(3):
        grad_copy(1, k).wait_recv()
        grad_copy(2, k).wait_recv()
        grad_ref[:, k * width : (k + 1) * width] = (
            part[k, r].astype(jnp.float32)
            + sib[1, k].astype(jnp.float32)
            + from_x[k].astype(jnp.float32)
        )
    for k in range(3):
        for kind in range(3):
            weight_copy(kind, k).wait_send()
            grad_copy(kind, k).wait_send()
    for b in range(batches):
        each_peer(lambda k: dispatch(0, b, k).wait_send())
        each_peer(lambda k: dispatch(1, b, k).wait_send())
        each_peer(lambda k: give_back(b, k).wait_send())


def fused_layer(experts, capacity, inputs, out_grads, routes, gate_probs, master):
    batches, tokens, width = inputs.shape
    units = master.shape[0]
    rows = experts * capacity
    peers = experts - 1
    low = jnp.bfloat16
    whole = pl.BlockSpec(memory_space=pltpu.VMEM)
    dma = pltpu.SemaphoreType.DMA
    return pl.pallas_call(
        functools.partial(layer_kernel, experts, capacity),
        out_shape=(
            jax.ShapeDtypeStruct(inputs.shape, low),
            jax.ShapeDtypeStruct(master.shape, jnp.float32),
        ),
        in_specs=[whole] * 5,
        out_specs=(whole, whole),
        scratch_shapes=[
            pltpu.VMEM((2, batches, experts, capacity, width), low),
            pltpu.VMEM((2, batches, experts, capacity, width), low),
            pltpu.VMEM((3, 4, units, width), low),
            pltpu.VMEM((batches, experts, capacity, width), low),
            pltpu.VMEM((batches, experts, capacity, width), low),
            pltpu.VMEM((batches, tokens, rows), low),
            pltpu.VMEM((3, 4 * units, batches * rows), low),
            pltpu.VMEM((3, 4, units, width), low),
            pltpu.VMEM((2, 3, units, width), low),
            pltpu.VMEM((3, units, width), low),
            pltpu.VMEM((3, units, width), low),
            dma((2, batches, peers)),
            dma((2, batches, peers)),
            dma((batches, peers)),
            dma((batches, peers)),
            dma((3, 3)),
            dma((3, 3)),
            dma((3, 3)),
            dma((3, 3)),
        ],
        compiler_params=pltpu.CompilerParams(
            collective_id=0, has_side_effects=True, vmem_limit_bytes=48 * 1024 * 1024
        ),
        cost_estimate=pl.CostEstimate(
            flops=2 * 8 * batches * rows * 4 * units * width,
            bytes_accessed=8 * master.size,
            transcendentals=0,
        ),
    )(inputs, out_grads, routes, gate_probs, master)


def on_device(inputs, out_grads, routes, gate_probs, master, moment, second):
    experts = lax.axis_size("expert")
    tokens = inputs.shape[1]
    capacity = max(2, 2 * tokens * routes.shape[2] // experts)
    fits = capacity % 16 == 0 and experts * capacity % 128 == 0
    if routes.shape[2] != 1 or lax.axis_size("replica") != 4 or not fits:
        return on_device_plain(inputs, out_grads, routes, gate_probs, master, moment, second)
    in_grads, grad_sum = fused_layer(
        experts, capacity, inputs, out_grads, routes, gate_probs, master[0]
    )
    new_master, new_moment, new_second = adamw_step(master[0], moment[0], second[0], grad_sum)
    return (in_grads, new_master[None], new_moment[None], new_second[None])


def solution(mesh):
    placed = (
        P(None, ("expert", "replica"), None),
        P(None, ("expert", "replica"), None),
        P(None, ("expert", "replica"), None),
        P(None, ("expert", "replica"), None),
        P("expert", "replica", None),
        P("expert", "replica", None),
        P("expert", "replica", None),
    )
    return jax.shard_map(
        on_device,
        mesh=mesh,
        in_specs=placed,
        out_specs=(
            P(None, ("expert", "replica"), None),
            P("expert", "replica", None),
            P("expert", "replica", None),
            P("expert", "replica", None),
        ),
        check_vma=False,
    )
```

```python
import functools
import math

import jax
import jax.numpy as jnp
from jax import lax
from jax.experimental import pallas as pl
from jax.experimental.pallas import tpu as pltpu
from jax.sharding import PartitionSpec as P

beta_one = 0.9
beta_two = 0.95
learning_rate = 0.01
decay_rate = 0.1
epsilon = 1e-08
MESH = pl.DeviceIdType.MESH
NT = (((1,), (1,)), ((), ()))


def slot_positions(route_pairs, capacity):
    pair_count = route_pairs.shape[-1]
    positions = jnp.arange(pair_count, dtype=jnp.int32)
    same_route = (route_pairs[..., :, None] == route_pairs[..., None, :]) & (
        positions[None, :] < positions[:, None]
    )
    earlier = jnp.sum(same_route.astype(jnp.int32), axis=-1)
    return route_pairs * capacity + earlier


def expert_rows(rows_in, rows_grad, weights):
    model_width = rows_in.shape[-1]
    scale_in = 1.0 / math.sqrt(model_width)
    scale_hidden = 1.0 / math.sqrt(weights.shape[0])
    w_gate = weights[:, :model_width]
    w_up = weights[:, model_width : 2 * model_width]
    w_down = weights[:, 2 * model_width :]
    gate_value = jnp.dot(rows_in, w_gate.T, preferred_element_type=jnp.float32) * scale_in
    up_value = jnp.dot(rows_in, w_up.T, preferred_element_type=jnp.float32) * scale_in
    sigmoid_gate = jax.nn.sigmoid(gate_value)
    activated = gate_value * sigmoid_gate
    hidden = (activated * up_value).astype(jnp.bfloat16)
    hidden_grad = jnp.dot(rows_grad, w_down.T, preferred_element_type=jnp.float32) * scale_hidden
    up_grad = (hidden_grad * activated).astype(jnp.bfloat16)
    gate_grad = (
        hidden_grad * up_value * sigmoid_gate * (1.0 + gate_value * (1.0 - sigmoid_gate))
    ).astype(jnp.bfloat16)
    slot_grads = (
        jnp.dot(gate_grad, w_gate, preferred_element_type=jnp.float32)
        + jnp.dot(up_grad, w_up, preferred_element_type=jnp.float32)
    ) * scale_in
    return (hidden, gate_grad, up_grad, slot_grads.astype(jnp.bfloat16))


def gate_up_terms(rows_in, gate_grad, up_grad):
    scale_in = 1.0 / math.sqrt(rows_in.shape[-1])
    gate_term = jnp.dot(gate_grad.T, rows_in, preferred_element_type=jnp.float32) * scale_in
    up_term = jnp.dot(up_grad.T, rows_in, preferred_element_type=jnp.float32) * scale_in
    return jnp.concatenate([gate_term, up_term], axis=1)


def down_terms(rows_grad, hidden):
    scale_hidden = 1.0 / math.sqrt(hidden.shape[-1])
    return jnp.dot(hidden.T, rows_grad, preferred_element_type=jnp.float32) * scale_hidden


def adamw_step(master, moment, second, grad_sum):
    new_moment = beta_one * moment + (1.0 - beta_one) * grad_sum
    second_sum = beta_two * second.astype(jnp.float32) + (1.0 - beta_two) * grad_sum * grad_sum
    new_master = master - learning_rate * (
        new_moment / (jnp.sqrt(second_sum) + epsilon) + decay_rate * master
    )
    return (new_master, new_moment, second_sum.astype(jnp.bfloat16))


def on_device_plain(inputs, out_grads, routes, gate_probs, master, moment, second):
    experts = lax.axis_size("expert")
    batches, tokens, model_width = inputs.shape
    top_count = routes.shape[2]
    pair_count = tokens * top_count
    capacity = max(2, 2 * pair_count // experts)
    weights = lax.all_gather(master[0].astype(jnp.bfloat16), "replica", axis=0, tiled=True)
    route_pairs = routes.reshape(batches, pair_count)
    slot_ids = slot_positions(route_pairs, capacity)
    slot_range = jnp.arange(experts * capacity, dtype=jnp.int32)
    onehot = (slot_ids[:, None, :] == slot_range[None, :, None]).astype(jnp.bfloat16)
    onehot = onehot.reshape(batches, experts, capacity, pair_count)
    pair_inputs = jnp.repeat(inputs, top_count, axis=1)
    pair_grads = (
        gate_probs.reshape(batches, pair_count)[..., None]
        * jnp.repeat(out_grads, top_count, axis=1).astype(jnp.float32)
    ).astype(jnp.bfloat16)
    send_in = jnp.einsum(
        "besp,bpd->ebsd", onehot, pair_inputs, preferred_element_type=jnp.float32
    ).astype(jnp.bfloat16)
    send_grad = jnp.einsum(
        "besp,bpd->ebsd", onehot, pair_grads, preferred_element_type=jnp.float32
    ).astype(jnp.bfloat16)
    arrived_in, arrived_grad = (
        lax.all_to_all(send_in, "expert", split_axis=0, concat_axis=0, tiled=True),
        lax.all_to_all(send_grad, "expert", split_axis=0, concat_axis=0, tiled=True),
    )
    all_in = arrived_in.reshape(experts * batches * capacity, model_width)
    all_grad = arrived_grad.reshape(experts * batches * capacity, model_width)
    all_hidden, all_gate, all_up, slot_grads = expert_rows(all_in, all_grad, weights)
    returned_rows = lax.all_to_all(
        slot_grads.reshape(experts, batches, capacity, model_width),
        "expert",
        split_axis=0,
        concat_axis=0,
        tiled=True,
    )
    pair_back = jnp.einsum(
        "besp,ebsd->bpd", onehot, returned_rows, preferred_element_type=jnp.float32
    )
    in_grads = jnp.sum(pair_back.reshape(batches, tokens, top_count, model_width), axis=2).astype(
        jnp.bfloat16
    )
    grad_sum = lax.psum_scatter(
        jnp.concatenate(
            [gate_up_terms(all_in, all_gate, all_up), down_terms(all_grad, all_hidden)], axis=1
        ).astype(jnp.bfloat16),
        "replica",
        scatter_dimension=0,
        tiled=True,
    ).astype(jnp.float32)
    new_master, new_moment, new_second = adamw_step(master[0], moment[0], second[0], grad_sum)
    return (in_grads, new_master[None], new_moment[None], new_second[None])


def layer_kernel(
    experts,
    capacity,
    in_ref,
    og_ref,
    routes_ref,
    probs_ref,
    master_ref,
    ingrad_ref,
    grad_ref,
    held_in,
    held_og,
    held_master,
    send,
    recv,
    weights,
    slots,
    ret,
    pick_back,
    terms,
    part,
    sib,
    chip_sum,
    from_x,
    dsend,
    drecv,
    bsend,
    brecv,
    wsend,
    wrecv,
    rsend,
    rrecv,
    load_sem,
):
    batches, tokens, width = in_ref.shape
    units = weights.shape[2]
    total_units = 4 * units
    rows = experts * capacity
    scale_in = 1.0 / math.sqrt(width)
    scale_hidden = 1.0 / math.sqrt(total_units)
    e = lax.axis_index("expert")
    r = lax.axis_index("replica")
    chip_x, core = r // 2, lax.rem(r, 2)
    r_sib = chip_x * 2 + (1 - core)
    r_x = (1 - chip_x) * 2 + core
    r_far = (1 - chip_x) * 2 + (1 - core)

    loads_in = [
        pltpu.make_async_copy(in_ref.at[b], held_in.at[b], load_sem.at[0, b])
        for b in range(batches)
    ]
    loads_og = [
        pltpu.make_async_copy(og_ref.at[b], held_og.at[b], load_sem.at[1, b])
        for b in range(batches)
    ]
    load_master = pltpu.make_async_copy(master_ref, held_master, load_sem.at[2, 0])
    loads_in[0].start()

    barrier = pltpu.get_barrier_semaphore()

    def greet(k, c):
        pl.semaphore_signal(
            barrier, inc=1, device_id=(lax.rem(e + k, experts), r), device_id_type=MESH
        )
        return c

    lax.fori_loop(1, experts, greet, 0)
    for other in (r_sib, r_x):
        pl.semaphore_signal(barrier, inc=1, device_id=(e, other), device_id_type=MESH)
    load_master.start()
    loads_og[0].start()
    for b in range(1, batches):
        loads_in[b].start()
        loads_og[b].start()

    def dispatch(which, b, k):
        peer = lax.rem(e + k, experts)
        return pltpu.make_async_remote_copy(
            src_ref=send.at[which, b, peer],
            dst_ref=recv.at[which, b, e],
            send_sem=dsend.at[which, b, k - 1],
            recv_sem=drecv.at[which, b, k - 1],
            device_id=(peer, r),
            device_id_type=MESH,
        )

    def give_back(b, k):
        peer = lax.rem(e + k, experts)
        return pltpu.make_async_remote_copy(
            src_ref=slots.at[b, peer],
            dst_ref=ret.at[b, e],
            send_sem=bsend.at[b, k - 1],
            recv_sem=brecv.at[b, k - 1],
            device_id=(peer, r),
            device_id_type=MESH,
        )

    def weight_copy(kind, k):
        block = (r, r, r_x)[kind]
        target = (r_sib, r_x, r_sib)[kind]
        return pltpu.make_async_remote_copy(
            src_ref=weights.at[k, block],
            dst_ref=weights.at[k, block],
            send_sem=wsend.at[kind, k],
            recv_sem=wrecv.at[kind, k],
            device_id=(e, target),
            device_id_type=MESH,
        )

    def grad_copy(kind, k):
        if kind == 2:
            source, target, place = chip_sum.at[k], r_x, from_x.at[k]
        else:
            source, target = part.at[k, (r_far, r_sib)[kind]], r_sib
            place = sib.at[kind, k]
        return pltpu.make_async_remote_copy(
            src_ref=source,
            dst_ref=place,
            send_sem=rsend.at[kind, k],
            recv_sem=rrecv.at[kind, k],
            device_id=(e, target),
            device_id_type=MESH,
        )

    def each_peer(step):
        def body(k, c):
            step(k)
            return c

        lax.fori_loop(1, experts, body, 0)

    first = lax.broadcasted_iota(jnp.int32, (tokens, tokens), 0)
    second = lax.broadcasted_iota(jnp.int32, (tokens, tokens), 1)

    def pick(b):
        route_row = routes_ref[b].astype(jnp.float32)
        route_col = jnp.sum(jnp.where(first == second, route_row, 0.0), axis=1, keepdims=True)
        same = route_col == route_row
        before_row = jnp.sum(
            jnp.where(same & (first < second), 1.0, 0.0), axis=0, keepdims=True
        )
        before_col = jnp.sum(
            jnp.where(same & (second < first), 1.0, 0.0), axis=1, keepdims=True
        )
        slot_row = route_row * capacity + before_row
        slot_col = route_col * capacity + before_col
        by_slot = lax.broadcasted_iota(jnp.int32, (rows, tokens), 0).astype(jnp.float32)
        by_token = lax.broadcasted_iota(jnp.int32, (tokens, rows), 1).astype(jnp.float32)
        one_hot = jnp.where(by_slot == slot_row, 1.0, 0.0).astype(jnp.bfloat16)
        pick_back[b] = jnp.where(by_token == slot_col, 1.0, 0.0).astype(jnp.bfloat16)
        return one_hot

    def fill(which, b, one_hot):
        if which == 0:
            loads_in[b].wait()
            source = held_in[b]
        else:
            probs = jnp.sum(jnp.where(first == second, probs_ref[b], 0.0), axis=1, keepdims=True)
            loads_og[b].wait()
            source = (probs * held_og[b].astype(jnp.float32)).astype(jnp.bfloat16)
        chosen = jnp.dot(one_hot, source, preferred_element_type=jnp.float32)
        send[which, b] = chosen.astype(jnp.bfloat16).reshape(experts, capacity, width)
        recv[which, b, e] = send[which, b, e]

    one_hot = pick(0)
    fill(0, 0, one_hot)
    pl.semaphore_wait(barrier, experts + 1)
    each_peer(lambda k: dispatch(0, 0, k).start())
    load_master.wait()
    for k in range(3):
        weights[k, r] = held_master[:, k * width : (k + 1) * width].astype(jnp.bfloat16)
        weight_copy(1, k).start()
        weight_copy(0, k).start()
    fill(1, 0, one_hot)
    each_peer(lambda k: dispatch(1, 0, k).start())
    for b in range(1, batches):
        one_hot = pick(b)
        for which in range(2):
            fill(which, b, one_hot)
            each_peer(lambda k: dispatch(which, b, k).start())

    for k in range(3):
        weight_copy(1, k).wait_recv()
        weight_copy(2, k).start()
    for k in range(3):
        weight_copy(0, k).wait_recv()
        weight_copy(2, k).wait_recv()

    def matrix(k):
        return weights[k].reshape(total_units, width)

    def weight_grad(k):
        source = recv[k // 2].reshape(batches * rows, width)
        total = jnp.dot(terms[k], source, preferred_element_type=jnp.float32)
        total = total * (scale_hidden if k == 2 else scale_in)
        part[k] = total.astype(jnp.bfloat16).reshape(4, units, width)
        grad_copy(0, k).start()
        grad_copy(1, k).start()

    def over_x(k):
        grad_copy(0, k).wait_recv()
        chip_sum[k] = (
            part[k, r_x].astype(jnp.float32) + sib[0, k].astype(jnp.float32)
        ).astype(jnp.bfloat16)
        grad_copy(2, k).start()

    for b in range(batches):
        last = b == batches - 1
        span = slice(b * rows, (b + 1) * rows)
        each_peer(lambda k: dispatch(0, b, k).wait_recv())
        x = recv[0, b].reshape(rows, width)
        gate = lax.dot_general(x, matrix(0), NT, preferred_element_type=jnp.float32) * scale_in
        up = lax.dot_general(x, matrix(1), NT, preferred_element_type=jnp.float32) * scale_in
        sig = jax.nn.sigmoid(gate)
        act = gate * sig
        terms[2, :, span] = (act * up).T.astype(jnp.bfloat16)
        each_peer(lambda k: dispatch(1, b, k).wait_recv())
        if last:
            for done in range(b):
                each_peer(lambda k: give_back(done, k).start())
            weight_grad(2)
        g = recv[1, b].reshape(rows, width)
        hgrad = (
            lax.dot_general(g, matrix(2), NT, preferred_element_type=jnp.float32) * scale_hidden
        )
        up_grad = hgrad * act
        gate_grad = hgrad * up * sig * (1.0 + gate * (1.0 - sig))
        terms[0, :, span] = gate_grad.T.astype(jnp.bfloat16)
        terms[1, :, span] = up_grad.T.astype(jnp.bfloat16)
        if last:
            over_x(2)
            weight_grad(0)
            weight_grad(1)
            over_x(0)
        back = (
            jnp.dot(gate_grad.astype(jnp.bfloat16), matrix(0), preferred_element_type=jnp.float32)
            + jnp.dot(up_grad.astype(jnp.bfloat16), matrix(1), preferred_element_type=jnp.float32)
        ) * scale_in
        slots[b] = back.astype(jnp.bfloat16).reshape(experts, capacity, width)
        ret[b, e] = slots[b, e]
        if last:
            each_peer(lambda k: give_back(b, k).start())
            over_x(1)

    for b in range(batches):
        each_peer(lambda k: give_back(b, k).wait_recv())
        back = jnp.dot(
            pick_back[b], ret[b].reshape(rows, width), preferred_element_type=jnp.float32
        )
        ingrad_ref[b] = back.astype(jnp.bfloat16)
    for k in range(3):
        grad_copy(1, k).wait_recv()
        grad_copy(2, k).wait_recv()
        grad_ref[:, k * width : (k + 1) * width] = (
            part[k, r].astype(jnp.float32)
            + sib[1, k].astype(jnp.float32)
            + from_x[k].astype(jnp.float32)
        )
    for k in range(3):
        for kind in range(3):
            weight_copy(kind, k).wait_send()
            grad_copy(kind, k).wait_send()
    for b in range(batches):
        each_peer(lambda k: dispatch(0, b, k).wait_send())
        each_peer(lambda k: dispatch(1, b, k).wait_send())
        each_peer(lambda k: give_back(b, k).wait_send())


def fused_layer(experts, capacity, inputs, out_grads, routes, gate_probs, master):
    batches, tokens, width = inputs.shape
    units = master.shape[0]
    rows = experts * capacity
    peers = experts - 1
    low = jnp.bfloat16
    whole = pl.BlockSpec(memory_space=pltpu.VMEM)
    far = pl.BlockSpec(memory_space=pltpu.HBM)
    dma = pltpu.SemaphoreType.DMA
    return pl.pallas_call(
        functools.partial(layer_kernel, experts, capacity),
        out_shape=(
            jax.ShapeDtypeStruct(inputs.shape, low),
            jax.ShapeDtypeStruct(master.shape, jnp.float32),
        ),
        in_specs=[far, far, whole, whole, far],
        out_specs=(whole, whole),
        scratch_shapes=[
            pltpu.VMEM(inputs.shape, low),
            pltpu.VMEM(inputs.shape, low),
            pltpu.VMEM(master.shape, jnp.float32),
            pltpu.VMEM((2, batches, experts, capacity, width), low),
            pltpu.VMEM((2, batches, experts, capacity, width), low),
            pltpu.VMEM((3, 4, units, width), low),
            pltpu.VMEM((batches, experts, capacity, width), low),
            pltpu.VMEM((batches, experts, capacity, width), low),
            pltpu.VMEM((batches, tokens, rows), low),
            pltpu.VMEM((3, 4 * units, batches * rows), low),
            pltpu.VMEM((3, 4, units, width), low),
            pltpu.VMEM((2, 3, units, width), low),
            pltpu.VMEM((3, units, width), low),
            pltpu.VMEM((3, units, width), low),
            dma((2, batches, peers)),
            dma((2, batches, peers)),
            dma((batches, peers)),
            dma((batches, peers)),
            dma((3, 3)),
            dma((3, 3)),
            dma((3, 3)),
            dma((3, 3)),
            dma((3, batches)),
        ],
        compiler_params=pltpu.CompilerParams(
            collective_id=0, has_side_effects=True, vmem_limit_bytes=61 * 1024 * 1024
        ),
        cost_estimate=pl.CostEstimate(
            flops=2 * 8 * batches * rows * 4 * units * width,
            bytes_accessed=8 * master.size,
            transcendentals=0,
        ),
    )(
        inputs,
        out_grads,
        routes.reshape(batches, 1, tokens),
        gate_probs.reshape(batches, 1, tokens),
        master,
    )


def update_kernel(
    ingrad_in, grad, master, moment, second, ingrad, nmaster, nmoment, nsecond, *scratch
):
    held, made, sems = scratch[:4], scratch[4:7], scratch[7]
    depth = 16
    pieces = grad.shape[0] // depth
    spans = [pl.ds(i * depth, depth) for i in range(pieces)]
    loads = [
        [
            pltpu.make_async_copy(source.at[span], place.at[span], sems.at[n, i])
            for n, (source, place) in enumerate(zip((grad, master, moment, second), held))
        ]
        for i, span in enumerate(spans)
    ]
    for piece in loads:
        for load in piece:
            load.start()
    rows_in = pltpu.make_async_copy(ingrad_in, scratch[8], sems.at[7, 0])
    rows_in.start()
    copies = []
    for i, span in enumerate(spans):
        for load in loads[i]:
            load.wait()
        values = adamw_step(held[1][span], held[2][span], held[3][span], held[0][span])
        for n, target in enumerate((nmaster, nmoment, nsecond)):
            made[n][span] = values[n]
            copies.append(
                pltpu.make_async_copy(made[n].at[span], target.at[span], sems.at[4 + n, i])
            )
            copies[-1].start()
    rows_in.wait()
    copies.append(pltpu.make_async_copy(scratch[8], ingrad, sems.at[7, 1]))
    copies[-1].start()
    for copy in copies:
        copy.wait()


def update(in_grads, grad_sum, master, moment, second):
    far = pl.BlockSpec(memory_space=pltpu.HBM)
    outs = [in_grads, master, moment, second]
    return pl.pallas_call(
        update_kernel,
        out_shape=tuple(jax.ShapeDtypeStruct(o.shape, o.dtype) for o in outs),
        in_specs=[far] * 5,
        out_specs=(far,) * 4,
        scratch_shapes=[
            pltpu.VMEM(o.shape, o.dtype)
            for o in (grad_sum, master, moment, second, master, moment, second)
        ]
        + [
            pltpu.SemaphoreType.DMA((8, max(2, master.shape[0] // 16))),
            pltpu.VMEM(in_grads.shape, in_grads.dtype),
        ],
        compiler_params=pltpu.CompilerParams(vmem_limit_bytes=61 * 1024 * 1024),
        cost_estimate=pl.CostEstimate(
            flops=16 * master.size, bytes_accessed=20 * master.size, transcendentals=master.size
        ),
    )(in_grads, grad_sum, master, moment, second)


def on_device(inputs, out_grads, routes, gate_probs, master, moment, second):
    experts = lax.axis_size("expert")
    tokens = inputs.shape[1]
    capacity = max(2, 2 * tokens * routes.shape[2] // experts)
    fits = capacity % 16 == 0 and master.shape[1] % 16 == 0 and experts * capacity % 128 == 0
    if routes.shape[2] != 1 or lax.axis_size("replica") != 4 or not fits:
        return on_device_plain(inputs, out_grads, routes, gate_probs, master, moment, second)
    in_grads, grad_sum = fused_layer(
        experts, capacity, inputs, out_grads, routes, gate_probs, master[0]
    )
    in_grads, new_master, new_moment, new_second = update(
        in_grads, grad_sum, master[0], moment[0], second[0]
    )
    return (in_grads, new_master[None], new_moment[None], new_second[None])


def solution(mesh):
    placed = (
        P(None, ("expert", "replica"), None),
        P(None, ("expert", "replica"), None),
        P(None, ("expert", "replica"), None),
        P(None, ("expert", "replica"), None),
        P("expert", "replica", None),
        P("expert", "replica", None),
        P("expert", "replica", None),
    )
    return jax.shard_map(
        on_device,
        mesh=mesh,
        in_specs=placed,
        out_specs=(
            P(None, ("expert", "replica"), None),
            P("expert", "replica", None),
            P("expert", "replica", None),
            P("expert", "replica", None),
        ),
        check_vma=False,
    )
```

```python
import functools
import math

import jax
import jax.numpy as jnp
from jax import lax
from jax.experimental import pallas as pl
from jax.experimental.pallas import tpu as pltpu
from jax.sharding import PartitionSpec as P

beta_one = 0.9
beta_two = 0.95
learning_rate = 0.01
decay_rate = 0.1
epsilon = 1e-08
MESH = pl.DeviceIdType.MESH
NT = (((1,), (1,)), ((), ()))


def slot_positions(route_pairs, capacity):
    pair_count = route_pairs.shape[-1]
    positions = jnp.arange(pair_count, dtype=jnp.int32)
    same_route = (route_pairs[..., :, None] == route_pairs[..., None, :]) & (
        positions[None, :] < positions[:, None]
    )
    earlier = jnp.sum(same_route.astype(jnp.int32), axis=-1)
    return route_pairs * capacity + earlier


def expert_rows(rows_in, rows_grad, weights):
    model_width = rows_in.shape[-1]
    scale_in = 1.0 / math.sqrt(model_width)
    scale_hidden = 1.0 / math.sqrt(weights.shape[0])
    w_gate = weights[:, :model_width]
    w_up = weights[:, model_width : 2 * model_width]
    w_down = weights[:, 2 * model_width :]
    gate_value = jnp.dot(rows_in, w_gate.T, preferred_element_type=jnp.float32) * scale_in
    up_value = jnp.dot(rows_in, w_up.T, preferred_element_type=jnp.float32) * scale_in
    sigmoid_gate = jax.nn.sigmoid(gate_value)
    activated = gate_value * sigmoid_gate
    hidden = (activated * up_value).astype(jnp.bfloat16)
    hidden_grad = jnp.dot(rows_grad, w_down.T, preferred_element_type=jnp.float32) * scale_hidden
    up_grad = (hidden_grad * activated).astype(jnp.bfloat16)
    gate_grad = (
        hidden_grad * up_value * sigmoid_gate * (1.0 + gate_value * (1.0 - sigmoid_gate))
    ).astype(jnp.bfloat16)
    slot_grads = (
        jnp.dot(gate_grad, w_gate, preferred_element_type=jnp.float32)
        + jnp.dot(up_grad, w_up, preferred_element_type=jnp.float32)
    ) * scale_in
    return (hidden, gate_grad, up_grad, slot_grads.astype(jnp.bfloat16))


def gate_up_terms(rows_in, gate_grad, up_grad):
    scale_in = 1.0 / math.sqrt(rows_in.shape[-1])
    gate_term = jnp.dot(gate_grad.T, rows_in, preferred_element_type=jnp.float32) * scale_in
    up_term = jnp.dot(up_grad.T, rows_in, preferred_element_type=jnp.float32) * scale_in
    return jnp.concatenate([gate_term, up_term], axis=1)


def down_terms(rows_grad, hidden):
    scale_hidden = 1.0 / math.sqrt(hidden.shape[-1])
    return jnp.dot(hidden.T, rows_grad, preferred_element_type=jnp.float32) * scale_hidden


def adamw_step(master, moment, second, grad_sum):
    new_moment = beta_one * moment + (1.0 - beta_one) * grad_sum
    second_sum = beta_two * second.astype(jnp.float32) + (1.0 - beta_two) * grad_sum * grad_sum
    new_master = master - learning_rate * (
        new_moment / (jnp.sqrt(second_sum) + epsilon) + decay_rate * master
    )
    return (new_master, new_moment, second_sum.astype(jnp.bfloat16))


def on_device_plain(inputs, out_grads, routes, gate_probs, master, moment, second):
    experts = lax.axis_size("expert")
    batches, tokens, model_width = inputs.shape
    top_count = routes.shape[2]
    pair_count = tokens * top_count
    capacity = max(2, 2 * pair_count // experts)
    weights = lax.all_gather(master[0].astype(jnp.bfloat16), "replica", axis=0, tiled=True)
    route_pairs = routes.reshape(batches, pair_count)
    slot_ids = slot_positions(route_pairs, capacity)
    slot_range = jnp.arange(experts * capacity, dtype=jnp.int32)
    onehot = (slot_ids[:, None, :] == slot_range[None, :, None]).astype(jnp.bfloat16)
    onehot = onehot.reshape(batches, experts, capacity, pair_count)
    pair_inputs = jnp.repeat(inputs, top_count, axis=1)
    pair_grads = (
        gate_probs.reshape(batches, pair_count)[..., None]
        * jnp.repeat(out_grads, top_count, axis=1).astype(jnp.float32)
    ).astype(jnp.bfloat16)
    send_in = jnp.einsum(
        "besp,bpd->ebsd", onehot, pair_inputs, preferred_element_type=jnp.float32
    ).astype(jnp.bfloat16)
    send_grad = jnp.einsum(
        "besp,bpd->ebsd", onehot, pair_grads, preferred_element_type=jnp.float32
    ).astype(jnp.bfloat16)
    arrived_in, arrived_grad = (
        lax.all_to_all(send_in, "expert", split_axis=0, concat_axis=0, tiled=True),
        lax.all_to_all(send_grad, "expert", split_axis=0, concat_axis=0, tiled=True),
    )
    all_in = arrived_in.reshape(experts * batches * capacity, model_width)
    all_grad = arrived_grad.reshape(experts * batches * capacity, model_width)
    all_hidden, all_gate, all_up, slot_grads = expert_rows(all_in, all_grad, weights)
    returned_rows = lax.all_to_all(
        slot_grads.reshape(experts, batches, capacity, model_width),
        "expert",
        split_axis=0,
        concat_axis=0,
        tiled=True,
    )
    pair_back = jnp.einsum(
        "besp,ebsd->bpd", onehot, returned_rows, preferred_element_type=jnp.float32
    )
    in_grads = jnp.sum(pair_back.reshape(batches, tokens, top_count, model_width), axis=2).astype(
        jnp.bfloat16
    )
    grad_sum = lax.psum_scatter(
        jnp.concatenate(
            [gate_up_terms(all_in, all_gate, all_up), down_terms(all_grad, all_hidden)], axis=1
        ).astype(jnp.bfloat16),
        "replica",
        scatter_dimension=0,
        tiled=True,
    ).astype(jnp.float32)
    new_master, new_moment, new_second = adamw_step(master[0], moment[0], second[0], grad_sum)
    return (in_grads, new_master[None], new_moment[None], new_second[None])


def layer_kernel(
    experts,
    capacity,
    in_ref,
    og_ref,
    routes_ref,
    probs_ref,
    master_ref,
    ingrad_ref,
    grad_ref,
    held_in,
    held_og,
    held_master,
    send,
    recv,
    weights,
    slots,
    ret,
    pick_back,
    terms,
    part,
    sib,
    chip_sum,
    from_x,
    dsend,
    drecv,
    bsend,
    brecv,
    wsend,
    wrecv,
    rsend,
    rrecv,
    load_sem,
):
    batches, tokens, width = in_ref.shape
    units = weights.shape[2]
    total_units = 4 * units
    rows = experts * capacity
    scale_in = 1.0 / math.sqrt(width)
    scale_hidden = 1.0 / math.sqrt(total_units)
    e = lax.axis_index("expert")
    r = lax.axis_index("replica")
    chip_x, core = r // 2, lax.rem(r, 2)
    r_sib = chip_x * 2 + (1 - core)
    r_x = (1 - chip_x) * 2 + core
    r_far = (1 - chip_x) * 2 + (1 - core)

    loads_in = [
        pltpu.make_async_copy(in_ref.at[b], held_in.at[b], load_sem.at[0, b])
        for b in range(batches)
    ]
    loads_og = [
        pltpu.make_async_copy(og_ref.at[b], held_og.at[b], load_sem.at[1, b])
        for b in range(batches)
    ]
    load_master = pltpu.make_async_copy(master_ref, held_master, load_sem.at[2, 0])
    loads_in[0].start()

    barrier = pltpu.get_barrier_semaphore()

    def greet(k, c):
        pl.semaphore_signal(
            barrier, inc=1, device_id=(lax.rem(e + k, experts), r), device_id_type=MESH
        )
        return c

    lax.fori_loop(1, experts, greet, 0)
    for other in (r_sib, r_x):
        pl.semaphore_signal(barrier, inc=1, device_id=(e, other), device_id_type=MESH)
    load_master.start()
    loads_og[0].start()
    for b in range(1, batches):
        loads_in[b].start()
        loads_og[b].start()

    def dispatch(which, b, k):
        peer = lax.rem(e + k, experts)
        return pltpu.make_async_remote_copy(
            src_ref=send.at[which, b, peer],
            dst_ref=recv.at[which, b, e],
            send_sem=dsend.at[which, b, k - 1],
            recv_sem=drecv.at[which, b, k - 1],
            device_id=(peer, r),
            device_id_type=MESH,
        )

    def give_back(b, k):
        peer = lax.rem(e + k, experts)
        return pltpu.make_async_remote_copy(
            src_ref=slots.at[b, peer],
            dst_ref=ret.at[b, e],
            send_sem=bsend.at[b, k - 1],
            recv_sem=brecv.at[b, k - 1],
            device_id=(peer, r),
            device_id_type=MESH,
        )

    def weight_copy(kind, k):
        block = (r, r, r_x)[kind]
        target = (r_sib, r_x, r_sib)[kind]
        return pltpu.make_async_remote_copy(
            src_ref=weights.at[k, block],
            dst_ref=weights.at[k, block],
            send_sem=wsend.at[kind, k],
            recv_sem=wrecv.at[kind, k],
            device_id=(e, target),
            device_id_type=MESH,
        )

    def grad_copy(kind, k):
        if kind == 2:
            source, target, place = chip_sum.at[k], r_x, from_x.at[k]
        else:
            source, target = part.at[k, (r_far, r_sib)[kind]], r_sib
            place = sib.at[kind, k]
        return pltpu.make_async_remote_copy(
            src_ref=source,
            dst_ref=place,
            send_sem=rsend.at[kind, k],
            recv_sem=rrecv.at[kind, k],
            device_id=(e, target),
            device_id_type=MESH,
        )

    def each_peer(step):
        def body(k, c):
            step(lax.rem(k, 2) * ((k + 1) // 2) + (1 - lax.rem(k, 2)) * (experts - k // 2))
            return c

        lax.fori_loop(1, experts, body, 0)

    first = lax.broadcasted_iota(jnp.int32, (tokens, tokens), 0)
    second = lax.broadcasted_iota(jnp.int32, (tokens, tokens), 1)

    def pick(b):
        route_row = routes_ref[b].astype(jnp.float32)
        route_col = jnp.sum(jnp.where(first == second, route_row, 0.0), axis=1, keepdims=True)
        same = route_col == route_row
        before_row = jnp.sum(
            jnp.where(same & (first < second), 1.0, 0.0), axis=0, keepdims=True
        )
        before_col = jnp.sum(
            jnp.where(same & (second < first), 1.0, 0.0), axis=1, keepdims=True
        )
        slot_row = route_row * capacity + before_row
        slot_col = route_col * capacity + before_col
        by_slot = lax.broadcasted_iota(jnp.int32, (rows, tokens), 0).astype(jnp.float32)
        by_token = lax.broadcasted_iota(jnp.int32, (tokens, rows), 1).astype(jnp.float32)
        one_hot = jnp.where(by_slot == slot_row, 1.0, 0.0).astype(jnp.bfloat16)
        pick_back[b] = jnp.where(by_token == slot_col, 1.0, 0.0).astype(jnp.bfloat16)
        return one_hot

    def fill(which, b, one_hot):
        if which == 0:
            loads_in[b].wait()
            source = held_in[b]
        else:
            probs = jnp.sum(jnp.where(first == second, probs_ref[b], 0.0), axis=1, keepdims=True)
            loads_og[b].wait()
            source = (probs * held_og[b].astype(jnp.float32)).astype(jnp.bfloat16)
        chosen = jnp.dot(one_hot, source, preferred_element_type=jnp.float32)
        send[which, b] = chosen.astype(jnp.bfloat16).reshape(experts, capacity, width)
        recv[which, b, e] = send[which, b, e]

    one_hot = pick(0)
    fill(0, 0, one_hot)
    pl.semaphore_wait(barrier, experts + 1)
    each_peer(lambda k: dispatch(0, 0, k).start())
    load_master.wait()
    for k in range(3):
        weights[k, r] = held_master[:, k * width : (k + 1) * width].astype(jnp.bfloat16)
        weight_copy(1, k).start()
        weight_copy(0, k).start()
    fill(1, 0, one_hot)
    each_peer(lambda k: dispatch(1, 0, k).start())
    for b in range(1, batches):
        one_hot = pick(b)
        for which in range(2):
            fill(which, b, one_hot)
            each_peer(lambda k: dispatch(which, b, k).start())

    for k in range(3):
        weight_copy(1, k).wait_recv()
        weight_copy(2, k).start()
    for k in range(3):
        weight_copy(0, k).wait_recv()
        weight_copy(2, k).wait_recv()

    def matrix(k):
        return weights[k].reshape(total_units, width)

    def weight_grad(k):
        source = recv[k // 2].reshape(batches * rows, width)
        total = jnp.dot(terms[k], source, preferred_element_type=jnp.float32)
        total = total * (scale_hidden if k == 2 else scale_in)
        part[k] = total.astype(jnp.bfloat16).reshape(4, units, width)
        grad_copy(0, k).start()
        grad_copy(1, k).start()

    def over_x(k):
        grad_copy(0, k).wait_recv()
        chip_sum[k] = (
            part[k, r_x].astype(jnp.float32) + sib[0, k].astype(jnp.float32)
        ).astype(jnp.bfloat16)
        grad_copy(2, k).start()

    for b in range(batches):
        last = b == batches - 1
        span = slice(b * rows, (b + 1) * rows)
        each_peer(lambda k: dispatch(0, b, k).wait_recv())
        x = recv[0, b].reshape(rows, width)
        gate = lax.dot_general(x, matrix(0), NT, preferred_element_type=jnp.float32) * scale_in
        up = lax.dot_general(x, matrix(1), NT, preferred_element_type=jnp.float32) * scale_in
        sig = jax.nn.sigmoid(gate)
        act = gate * sig
        terms[2, :, span] = (act * up).T.astype(jnp.bfloat16)
        each_peer(lambda k: dispatch(1, b, k).wait_recv())
        if last:
            for done in range(b):
                each_peer(lambda k: give_back(done, k).start())
            weight_grad(2)
        g = recv[1, b].reshape(rows, width)
        hgrad = (
            lax.dot_general(g, matrix(2), NT, preferred_element_type=jnp.float32) * scale_hidden
        )
        up_grad = hgrad * act
        gate_grad = hgrad * up * sig * (1.0 + gate * (1.0 - sig))
        terms[0, :, span] = gate_grad.T.astype(jnp.bfloat16)
        terms[1, :, span] = up_grad.T.astype(jnp.bfloat16)
        if last:
            over_x(2)
            weight_grad(0)
            weight_grad(1)
            over_x(0)
        back = (
            jnp.dot(gate_grad.astype(jnp.bfloat16), matrix(0), preferred_element_type=jnp.float32)
            + jnp.dot(up_grad.astype(jnp.bfloat16), matrix(1), preferred_element_type=jnp.float32)
        ) * scale_in
        slots[b] = back.astype(jnp.bfloat16).reshape(experts, capacity, width)
        ret[b, e] = slots[b, e]
        if last:
            each_peer(lambda k: give_back(b, k).start())
            over_x(1)

    for b in range(batches):
        each_peer(lambda k: give_back(b, k).wait_recv())
        back = jnp.dot(
            pick_back[b], ret[b].reshape(rows, width), preferred_element_type=jnp.float32
        )
        ingrad_ref[b] = back.astype(jnp.bfloat16)
    for k in range(3):
        grad_copy(1, k).wait_recv()
        grad_copy(2, k).wait_recv()
        grad_ref[:, k * width : (k + 1) * width] = (
            part[k, r].astype(jnp.float32)
            + sib[1, k].astype(jnp.float32)
            + from_x[k].astype(jnp.float32)
        )
    for k in range(3):
        for kind in range(3):
            weight_copy(kind, k).wait_send()
            grad_copy(kind, k).wait_send()
    for b in range(batches):
        each_peer(lambda k: dispatch(0, b, k).wait_send())
        each_peer(lambda k: dispatch(1, b, k).wait_send())
        each_peer(lambda k: give_back(b, k).wait_send())


def fused_layer(experts, capacity, inputs, out_grads, routes, gate_probs, master):
    batches, tokens, width = inputs.shape
    units = master.shape[0]
    rows = experts * capacity
    peers = experts - 1
    low = jnp.bfloat16
    whole = pl.BlockSpec(memory_space=pltpu.VMEM)
    far = pl.BlockSpec(memory_space=pltpu.HBM)
    dma = pltpu.SemaphoreType.DMA
    return pl.pallas_call(
        functools.partial(layer_kernel, experts, capacity),
        out_shape=(
            jax.ShapeDtypeStruct(inputs.shape, low),
            jax.ShapeDtypeStruct(master.shape, jnp.float32),
        ),
        in_specs=[far, far, whole, whole, far],
        out_specs=(whole, whole),
        scratch_shapes=[
            pltpu.VMEM(inputs.shape, low),
            pltpu.VMEM(inputs.shape, low),
            pltpu.VMEM(master.shape, jnp.float32),
            pltpu.VMEM((2, batches, experts, capacity, width), low),
            pltpu.VMEM((2, batches, experts, capacity, width), low),
            pltpu.VMEM((3, 4, units, width), low),
            pltpu.VMEM((batches, experts, capacity, width), low),
            pltpu.VMEM((batches, experts, capacity, width), low),
            pltpu.VMEM((batches, tokens, rows), low),
            pltpu.VMEM((3, 4 * units, batches * rows), low),
            pltpu.VMEM((3, 4, units, width), low),
            pltpu.VMEM((2, 3, units, width), low),
            pltpu.VMEM((3, units, width), low),
            pltpu.VMEM((3, units, width), low),
            dma((2, batches, peers)),
            dma((2, batches, peers)),
            dma((batches, peers)),
            dma((batches, peers)),
            dma((3, 3)),
            dma((3, 3)),
            dma((3, 3)),
            dma((3, 3)),
            dma((3, batches)),
        ],
        compiler_params=pltpu.CompilerParams(
            collective_id=0, has_side_effects=True, vmem_limit_bytes=61 * 1024 * 1024
        ),
        cost_estimate=pl.CostEstimate(
            flops=2 * 8 * batches * rows * 4 * units * width,
            bytes_accessed=8 * master.size,
            transcendentals=0,
        ),
    )(
        inputs,
        out_grads,
        routes.reshape(batches, 1, tokens),
        gate_probs.reshape(batches, 1, tokens),
        master,
    )


def update_kernel(
    ingrad_in, grad, master, moment, second, ingrad, nmaster, nmoment, nsecond, *scratch
):
    held, made, sems = scratch[:4], scratch[4:7], scratch[7]
    depth = 16
    pieces = grad.shape[0] // depth
    spans = [pl.ds(i * depth, depth) for i in range(pieces)]
    loads = [
        [
            pltpu.make_async_copy(source.at[span], place.at[span], sems.at[n, i])
            for n, (source, place) in enumerate(zip((grad, master, moment, second), held))
        ]
        for i, span in enumerate(spans)
    ]
    for piece in loads:
        for load in piece:
            load.start()
    rows_in = pltpu.make_async_copy(ingrad_in, scratch[8], sems.at[7, 0])
    rows_in.start()
    copies = []
    for i, span in enumerate(spans):
        for load in loads[i]:
            load.wait()
        values = adamw_step(held[1][span], held[2][span], held[3][span], held[0][span])
        for n, target in enumerate((nmaster, nmoment, nsecond)):
            made[n][span] = values[n]
            copies.append(
                pltpu.make_async_copy(made[n].at[span], target.at[span], sems.at[4 + n, i])
            )
            copies[-1].start()
    rows_in.wait()
    copies.append(pltpu.make_async_copy(scratch[8], ingrad, sems.at[7, 1]))
    copies[-1].start()
    for copy in copies:
        copy.wait()


def update(in_grads, grad_sum, master, moment, second):
    far = pl.BlockSpec(memory_space=pltpu.HBM)
    outs = [in_grads, master, moment, second]
    return pl.pallas_call(
        update_kernel,
        out_shape=tuple(jax.ShapeDtypeStruct(o.shape, o.dtype) for o in outs),
        in_specs=[far] * 5,
        out_specs=(far,) * 4,
        scratch_shapes=[
            pltpu.VMEM(o.shape, o.dtype)
            for o in (grad_sum, master, moment, second, master, moment, second)
        ]
        + [
            pltpu.SemaphoreType.DMA((8, max(2, master.shape[0] // 16))),
            pltpu.VMEM(in_grads.shape, in_grads.dtype),
        ],
        compiler_params=pltpu.CompilerParams(vmem_limit_bytes=61 * 1024 * 1024),
        cost_estimate=pl.CostEstimate(
            flops=16 * master.size, bytes_accessed=20 * master.size, transcendentals=master.size
        ),
    )(in_grads, grad_sum, master, moment, second)


def on_device(inputs, out_grads, routes, gate_probs, master, moment, second):
    experts = lax.axis_size("expert")
    tokens = inputs.shape[1]
    capacity = max(2, 2 * tokens * routes.shape[2] // experts)
    fits = capacity % 16 == 0 and master.shape[1] % 16 == 0 and experts * capacity % 128 == 0
    if routes.shape[2] != 1 or lax.axis_size("replica") != 4 or not fits:
        return on_device_plain(inputs, out_grads, routes, gate_probs, master, moment, second)
    in_grads, grad_sum = fused_layer(
        experts, capacity, inputs, out_grads, routes, gate_probs, master[0]
    )
    in_grads, new_master, new_moment, new_second = update(
        in_grads, grad_sum, master[0], moment[0], second[0]
    )
    return (in_grads, new_master[None], new_moment[None], new_second[None])


def solution(mesh):
    placed = (
        P(None, ("expert", "replica"), None),
        P(None, ("expert", "replica"), None),
        P(None, ("expert", "replica"), None),
        P(None, ("expert", "replica"), None),
        P("expert", "replica", None),
        P("expert", "replica", None),
        P("expert", "replica", None),
    )
    return jax.shard_map(
        on_device,
        mesh=mesh,
        in_specs=placed,
        out_specs=(
            P(None, ("expert", "replica"), None),
            P("expert", "replica", None),
            P("expert", "replica", None),
            P("expert", "replica", None),
        ),
        check_vma=False,
    )
```
